256 devices in a mesh: tile: 128 (over z, y, x_hi, core), chan: 2 (over x_lo).
Axes of the slice: x: 4 (x_hi: 2, x_lo: 2; x = x_hi * 2 + x_lo), y: 4, z: 8, core: 2. Of those that a mesh axis runs over, the one named last changes fastest.
Arguments:
- activation: float32 [64, 128, 4, 4, 128], P('chan', 'tile'), may hold values from -6 to 6
- out_grad: float32 [64, 128, 4, 4, 128], P('chan', 'tile'), may hold values from -6 to 6
- kernel: float32 [27, 64, 64], P(None, 'chan'), may hold values from -0.15625 to 0.15625
Outputs:
- input_grad: float32 [64, 128, 4, 4, 128], P('chan', 'tile')
- kernel_grad: float32 [27, 64, 64], P(None, 'chan')
The draws below stay inside these ranges and needn't reach their ends.
All inputs are finite; a program needn't handle non-finite values.
Results may differ from the reference program's by a relative error of at most 0.0003.
Values sent between devices are 32-bit elements; how exact they have to be, the bound alone decides.
No kernel may reach another device: no remote copies, remote signals or barrier semaphores. Data moves between devices by JAX's collectives and lax.ppermute only.
A program may use at most 128 MiB of HBM per device.

```python
import math
import jax
import jax.numpy as jnp
from jax import lax

CIN = 64
COUT = 64
TY = 4
BX = 4
SZ = 4
BY = 128
SX = 128
SY = 512
N_TILE = 128


def block_scale(rng, shape, pieces, smallest, largest):
    level = 1.0
    for position, parts in pieces:
        draws = jax.random.uniform(jax.random.fold_in(jax.random.fold_in(rng, 6), position), (parts,), jnp.float32, smallest / len(pieces), largest / len(pieces))
        level = level * jnp.repeat(jnp.exp(draws), shape[position] // parts).reshape((-1,) + (1,) * (len(shape) - 1 - position))
    return level


def noise(stream_key, extent, spread, bound, cuts=(), dtype=jnp.bfloat16):
    array = spread * jax.random.normal(stream_key, extent, jnp.float32)
    if cuts:
        array = array * block_scale(stream_key, extent, cuts, -0.22, 0.18)
    return jnp.clip(array, -bound, bound).astype(dtype)


def setup_inputs(seed: int = 0) -> dict:
    arg_keys = jax.random.split(jax.random.key(seed), 4)
    return {
        "activation": noise(arg_keys[0], (CIN, N_TILE, BX, SZ, BY), 1.0, 6.0, ((0, 2), (1, 128)), jnp.float32),
        "out_grad": noise(arg_keys[1], (COUT, N_TILE, BX, SZ, BY), 1.0, 6.0, ((0, 2), (1, 128)), jnp.float32),
        "kernel": noise(arg_keys[2], (27, COUT, CIN), (27 * COUT) ** -0.5, 0.15625, ((1, 2),), jnp.float32),
    }


def forward(activation, weights):
    return lax.conv_general_dilated(activation[None], weights, (1, 1, 1), 'SAME', dimension_numbers=('NCXZY', 'OIXZY', 'NCXZY'), precision=lax.Precision.HIGHEST)[0]

def to_slab(field):
    chans = field.shape[0]
    tiled = field.reshape(chans, N_TILE // TY, TY, BX, SZ, BY)
    return tiled.transpose(0, 1, 3, 4, 2, 5).reshape(chans, SX, SZ, SY)

def from_slab(field):
    chans = field.shape[0]
    tiled = field.reshape(chans, N_TILE // TY, BX, SZ, TY, BY)
    return tiled.transpose(0, 1, 4, 2, 3, 5).reshape(chans, N_TILE, BX, SZ, BY)

def reference(activation, out_grad, kernel):
    weights = kernel.reshape(3, 3, 3, COUT, CIN).transpose(3, 4, 0, 1, 2)
    result, pullback = jax.vjp(forward, to_slab(activation), weights)
    input_grad, weight_grad = pullback(to_slab(out_grad))
    kernel_grad = weight_grad.transpose(2, 3, 4, 0, 1).reshape(27, COUT, CIN)
    kernel_grad = kernel_grad * (1.0 / math.sqrt(SX * SZ * SY))
    return (from_slab(input_grad), kernel_grad)
```

```python
import math

import jax
import jax.numpy as jnp
from jax import lax
from jax.sharding import Mesh, PartitionSpec as P

TY = 4
FAR = ("z",)
NEAR = ("y", "xh", "c")
TILE = FAR + NEAR


def passed_along(value, axis, steps):
    count = lax.axis_size(axis)
    leading, last = (max(0, -steps), min(count, count - steps))
    return lax.ppermute(value, axis, [(source, source + steps) for source in range(leading, last)])


def rim_cells(field):
    column = lax.axis_index(TILE) % TY
    below = passed_along(field[:, -1:], TILE, TY)
    above = passed_along(field[:, :1], TILE, -TY)
    extended = jnp.concatenate([below, field, above], axis=1)
    left_keep = jnp.where(column > 0, 1.0, 0.0).astype(jnp.float32)
    right_keep = jnp.where(column < TY - 1, 1.0, 0.0).astype(jnp.float32)
    left_side = passed_along(extended[..., -1:], TILE, 1) * left_keep
    right_side = passed_along(extended[..., :1], TILE, -1) * right_keep
    widened = jnp.concatenate([left_side, extended, right_side], axis=3)
    return jnp.pad(widened, ((0, 0), (0, 0), (1, 1), (0, 0)))


def window(padded, start_x, start_z, start_y, row_count, depth, width):
    piece = padded[
        :, start_x : start_x + row_count, start_z : start_z + depth, start_y : start_y + width
    ]
    return piece.reshape(piece.shape[0], -1)


def filter_terms(grad_flat, act_padded, row_count, depth, width):
    result = []
    for shift_x in range(3):
        for shift_z in range(3):
            for shift_y in range(3):
                act_piece = window(act_padded, shift_x, shift_z, shift_y, row_count, depth, width)
                result.append(
                    lax.dot_general(
                        grad_flat,
                        act_piece,
                        (((1,), (1,)), ((), ())),
                        precision=lax.Precision.HIGHEST,
                        preferred_element_type=jnp.float32,
                    )
                )
    return jnp.stack(result)


def data_terms(weights, grad_padded, row_count, depth, width):
    total = jnp.zeros((weights.shape[2], row_count * depth * width), jnp.float32)
    for shift_x in range(3):
        for shift_z in range(3):
            for shift_y in range(3):
                index_tap = 9 * shift_x + 3 * shift_z + shift_y
                grad_piece = window(
                    grad_padded, 2 - shift_x, 2 - shift_z, 2 - shift_y, row_count, depth, width
                )
                total = total + lax.dot_general(
                    weights[index_tap],
                    grad_piece,
                    (((0,), (0,)), ((), ())),
                    precision=lax.Precision.HIGHEST,
                    preferred_element_type=jnp.float32,
                )
    return total


def summed_over_tiles(partial):
    near = lax.axis_size(NEAR)
    far = lax.axis_size(FAR)
    pieces = partial.reshape(near, -1, 128)
    pieces = lax.all_to_all(pieces, NEAR, 0, 0, tiled=True)
    piece = jnp.sum(pieces, axis=0)
    copies = lax.all_to_all(
        jnp.broadcast_to(piece[None], (far,) + piece.shape), FAR, 0, 0, tiled=True
    )
    piece = jnp.sum(copies, axis=0)
    whole = lax.all_to_all(
        jnp.broadcast_to(piece[None], (near,) + piece.shape), NEAR, 0, 0, tiled=True
    )
    return whole.reshape(partial.shape)


def body(activation, out_grad, kernel):
    act_local = activation[:, 0]
    grad_local = out_grad[:, 0]
    row_count, depth, width = (act_local.shape[1], act_local.shape[2], act_local.shape[3])
    cin_local = act_local.shape[0]
    voxels = row_count * lax.axis_size(TILE) * depth * width
    act_full = lax.all_gather(act_local, "chan", axis=0, tiled=True)
    act_padded = rim_cells(act_full)
    grad_flat = grad_local.reshape(grad_local.shape[0], -1)
    local_filter = filter_terms(grad_flat, act_padded, row_count, depth, width) * (
        1.0 / math.sqrt(voxels)
    )
    kernel_grad = summed_over_tiles(local_filter)
    grad_padded = rim_cells(grad_local)
    input_flat = lax.psum_scatter(
        data_terms(kernel, grad_padded, row_count, depth, width),
        "chan",
        scatter_dimension=0,
        tiled=True,
    )
    input_grad = input_flat.reshape(cin_local, 1, row_count, depth, width)
    return (input_grad, kernel_grad)


def solution(mesh):
    mesh = Mesh(mesh.devices.reshape(8, 4, 2, 2, 2), TILE + ("chan",))
    in_specs = (
        P("chan", TILE, None, None, None),
        P("chan", TILE, None, None, None),
        P(None, "chan", None),
    )
    out_specs = (P("chan", TILE, None, None, None), P(None, "chan", None))
    return jax.shard_map(body, mesh=mesh, in_specs=in_specs, out_specs=out_specs, check_vma=False)
```

```python
import jax
import jax.numpy as jnp
from jax import lax
from jax.experimental import pallas as pl
from jax.experimental.pallas import tpu as pltpu
from jax.sharding import Mesh, PartitionSpec as P

F32, BF16 = jnp.float32, jnp.bfloat16
ALONG_X = ("z", "y")
ALONG_Y = ("xh", "c")
TILE = ALONG_X + ALONG_Y
NEAR = ("y", "xh", "c")
FAR = "z"
CI = 32
NT = (((1,), (1,)), ((), ()))


def passed_along(value, axis, steps):
    count = lax.axis_size(axis)
    first, last = max(0, -steps), min(count, count - steps)
    return lax.ppermute(value, axis, [(s, s + steps) for s in range(first, last)])


def traded(value):
    return lax.ppermute(value, "chan", [(0, 1), (1, 0)])


def split(value):
    high = value.astype(BF16)
    return high, (value - high.astype(F32)).astype(BF16)


def edges_kernel(grad, first, last):
    lane = lax.broadcasted_iota(jnp.int32, (CI, 128), 1)
    heads = jnp.zeros((CI, 128), F32)
    tails = jnp.zeros((CI, 128), F32)
    for cell in range(16):
        tile = grad[pl.ds(cell, CI, stride=16), :]
        place = 4 + cell
        heads = jnp.where(lane == place, pltpu.roll(tile, place, 1), heads)
        tails = jnp.where(lane == place, pltpu.roll(tile, place + 1, 1), tails)
    first[...] = heads
    last[...] = tails


def rim(own, below, above, at):
    lane = lax.broadcasted_iota(jnp.int32, (CI, 128), 1)
    low = pltpu.roll(below, (128 - 16 - at) % 128, 1)
    high = pltpu.roll(above, (16 - at) % 128, 1)
    return jnp.where(lane < 4, low, jnp.where(lane >= 20, high, own))


def spread(grad, below, above, left, right, high, low):
    lane = lax.broadcasted_iota(jnp.int32, (CI, 128), 1)
    zero = jnp.zeros((CI, 128), BF16)
    for xp in range(6):
        for d in range(3):
            for ref in (high, low):
                ref[d, xp, :, 0:128] = zero
                ref[d, xp, :, 640:768] = zero
        for z in range(4):
            if xp == 0:
                tile = below[pl.ds(z, CI, stride=4), :]
            elif xp == 5:
                tile = above[pl.ds(z, CI, stride=4), :]
            else:
                tile = grad[pl.ds((xp - 1) * 4 + z, CI, stride=16), :]
            at = xp * 4 + z
            before = jnp.where(
                lane == 0, pltpu.roll(left, (128 - at) % 128, 1), pltpu.roll(tile, 1, 1)
            )
            after = jnp.where(
                lane == 127, pltpu.roll(right, 127 - at, 1), pltpu.roll(tile, 127, 1)
            )
            for d, value in ((0, after), (1, tile), (2, before)):
                high[d, xp, :, (z + 1) * 128 : (z + 2) * 128], low[
                    d, xp, :, (z + 1) * 128 : (z + 2) * 128
                ] = split(value)


def taps(ref, x):
    return jnp.concatenate(
        [
            ref[d, x + 2 - a, :, (2 - b) * 128 : (2 - b) * 128 + 512]
            for a in range(3)
            for b in range(3)
            for d in range(3)
        ],
        axis=0,
    )


def x_row(ref, x):
    return jnp.concatenate([ref[pl.ds(x * 4 + z, CI, stride=16), :] for z in range(4)], axis=1)


def filter_kernel(
    chan, own, other, grad, below, above, left, right, rims_below, rims_above, out, high, low
):
    spread(
        grad,
        below,
        above,
        rim(left[...], rims_below[...], rims_above[...], 0),
        rim(right[...], rims_below[...], rims_above[...], 64),
        high,
        low,
    )
    is_first = chan[0] == 0
    total = None
    for x in range(4):
        mine, theirs = x_row(own, x), x_row(other, x)
        act = jnp.concatenate(
            [jnp.where(is_first, mine, theirs), jnp.where(is_first, theirs, mine)], axis=0
        )
        act_high, act_low = split(act)
        both = jnp.concatenate([act_high, act_low], axis=0)
        p = lax.dot_general(taps(high, x), both, NT, preferred_element_type=F32)
        q = lax.dot_general(taps(low, x), act_high, NT, preferred_element_type=F32)
        part = p[:, :64] + p[:, 64:] + q
        total = part if total is None else total + part
    total = total * (1.0 / 512.0)
    for j in range(16):
        if j < 13:
            pair = [total[64 * j : 64 * j + 32], total[64 * j + 32 : 64 * j + 64]]
        elif j == 13:
            pair = [total[64 * j : 64 * j + 32], jnp.zeros((32, 64), F32)]
        else:
            pair = [jnp.zeros((32, 64), F32)] * 2
        out[32 * j : 32 * j + 32, :] = jnp.concatenate(pair, axis=1)


def data_kernel(chan, weights, high, low, kept, sent):
    w = weights[...].reshape(864, 64)
    w = jnp.where(chan[0] == 0, w, jnp.concatenate([w[:, 32:], w[:, :32]], axis=1))
    w_high = w.astype(BF16).astype(F32)
    both = jnp.concatenate([w_high, w - w_high], axis=1)
    both = jnp.concatenate([both, jnp.zeros((32, 128), F32)], axis=0)
    both = both.T.astype(BF16)[:, :864]
    for x in range(4):
        p = jnp.dot(both, taps(high, x), preferred_element_type=F32)
        q = jnp.dot(both[:64], taps(low, x), preferred_element_type=F32)
        result = p[:64] + p[64:] + q
        for z in range(4):
            tile = result[:, z * 128 : (z + 1) * 128]
            kept[pl.ds(x * 4 + z, CI, stride=16), :] = tile[:32]
            sent[pl.ds(x * 4 + z, CI, stride=16), :] = tile[32:]


def sum_kernel(copies, pieces, out):
    def run(values, result):
        total = values[0:32, :]
        for j in range(1, pieces):
            total = total + values[32 * j : 32 * j + 32, :]
        for j in range(copies):
            result[32 * j : 32 * j + 32, :] = total

    return run


def unpack_kernel(packed, out):
    for tap in range(27):
        half = 64 * (tap % 2)
        out[tap, :, :] = packed[32 * (tap // 2) : 32 * (tap // 2) + 32, half : half + 64]


VMEM = pl.BlockSpec(memory_space=pltpu.VMEM)
SMEM = pl.BlockSpec(memory_space=pltpu.SMEM)
PARAMS = pltpu.CompilerParams(vmem_limit_bytes=40 * 2**20)


def shape(*dims, dtype=F32):
    return jax.ShapeDtypeStruct(dims, dtype)


def call(kernel, outs, in_specs, flops=0, moved=0):
    return pl.pallas_call(
        kernel,
        out_shape=outs,
        in_specs=in_specs,
        out_specs=jax.tree.map(lambda _: VMEM, outs),
        compiler_params=PARAMS,
        cost_estimate=pl.CostEstimate(flops=flops, bytes_accessed=moved, transcendentals=0),
    )


def summed(values, copies):
    rows = values.shape[0]
    return call(sum_kernel(copies, rows // 32, None), shape(32 * copies, 128), [VMEM])(values)


def summed_over_tiles(partial):
    near, far = lax.axis_size(NEAR), lax.axis_size(FAR)
    pieces = lax.all_to_all(partial, NEAR, 0, 0, tiled=True)
    copies = lax.all_to_all(summed(pieces, far), FAR, 0, 0, tiled=True)
    return lax.all_to_all(summed(copies, near), NEAR, 0, 0, tiled=True)


def body(activation, out_grad, kernel):
    act = activation.reshape(512, 128)
    grad = out_grad.reshape(512, 128)
    chan = lax.axis_index("chan").astype(jnp.int32).reshape(1)
    other = traded(act)
    first, last = call(edges_kernel, (shape(CI, 128),) * 2, [VMEM])(grad)
    left = passed_along(last, ALONG_Y, 1)
    right = passed_along(first, ALONG_Y, -1)
    rows = grad.reshape(CI, 4, 4, 128)
    below = passed_along(rows[:, 3], ALONG_X, 1).reshape(128, 128)
    above = passed_along(rows[:, 0], ALONG_X, -1).reshape(128, 128)
    rims = jnp.concatenate([left[:, :64], right[:, :64]], axis=1)
    rims_below = passed_along(rims, ALONG_X, 1)
    rims_above = passed_along(rims, ALONG_X, -1)
    halves = shape(3, 6, CI, 768, dtype=BF16)
    partial, high, low = call(
        filter_kernel, (shape(512, 128), halves, halves), [SMEM] + [VMEM] * 9, 700_000_000, 1 << 22
    )(chan, act, other, grad, below, above, left, right, rims_below, rims_above)
    kept, sent = call(
        data_kernel, (shape(512, 128),) * 2, [SMEM] + [VMEM] * 3, 700_000_000, 1 << 22
    )(chan, kernel, high, low)
    input_grad = (kept + traded(sent)).reshape(activation.shape)
    packed = summed_over_tiles(partial)
    kernel_grad = call(unpack_kernel, shape(27, 32, 64), [VMEM])(packed)
    return (input_grad, kernel_grad)


def solution(mesh):
    mesh = Mesh(mesh.devices.reshape(8, 4, 2, 2, 2), TILE + ("chan",))
    field = P("chan", TILE, None, None, None)
    weights = P(None, "chan", None)
    return jax.shard_map(
        body,
        mesh=mesh,
        in_specs=(field, field, weights),
        out_specs=(field, weights),
        check_vma=False,
    )
```

```python
import jax
import jax.numpy as jnp
from jax import lax
from jax.experimental import pallas as pl
from jax.experimental.pallas import tpu as pltpu
from jax.sharding import Mesh, PartitionSpec as P

F32, BF16 = jnp.float32, jnp.bfloat16
ALONG_X = ("z", "y")
ALONG_Y = ("xh", "c")
TILE = ALONG_X + ALONG_Y
NEAR = ("y", "xh", "c")
FAR = "z"
CI = 32
NT = (((1,), (1,)), ((), ()))


def swapped(value, axis, first):
    count = lax.axis_size(axis)
    pairs = [(s, s + 1) for s in range(first, count - 1, 2)]
    return lax.ppermute(value, axis, pairs + [(t, s) for s, t in pairs])


def split(value):
    high = value.astype(BF16)
    return high, (value - high.astype(F32)).astype(BF16)


def edges_kernel(odd, core, grad, near_row, far_row, to_core, to_chip):
    lane = lax.broadcasted_iota(jnp.int32, (CI, 128), 1)
    heads = jnp.zeros((CI, 128), F32)
    tails = jnp.zeros((CI, 128), F32)
    for xp in range(6):
        for z in range(4):
            tile = extended(odd, grad, near_row, far_row, xp, z)
            at = 4 * xp + z
            heads = jnp.where(lane == at, pltpu.roll(tile, at, 1), heads)
            tails = jnp.where(lane == at, pltpu.roll(tile, at + 1, 1), tails)
    is_first = core[0] == 0
    to_core[...] = jnp.where(is_first, tails, heads)
    to_chip[...] = jnp.where(is_first, heads, tails)


def extended(odd, grad, near_row, far_row, xp, z):
    if 0 < xp < 5:
        return grad[pl.ds((xp - 1) * 4 + z, CI, stride=16), :]
    near = near_row[pl.ds(z, CI, stride=4), :]
    far = far_row[pl.ds(z, CI, stride=4), :]
    return jnp.where((odd[0] == 1) == (xp == 0), near, far)


def spread(odd, grad, near_row, far_row, left, right, high, low):
    lane = lax.broadcasted_iota(jnp.int32, (CI, 128), 1)
    zero = jnp.zeros((CI, 128), BF16)
    for xp in range(6):
        for d in range(3):
            for ref in (high, low):
                ref[d, xp, :, 0:128] = zero
                ref[d, xp, :, 640:768] = zero
        for z in range(4):
            tile = extended(odd, grad, near_row, far_row, xp, z)
            at = xp * 4 + z
            before = jnp.where(
                lane == 0, pltpu.roll(left, (128 - at) % 128, 1), pltpu.roll(tile, 1, 1)
            )
            after = jnp.where(
                lane == 127, pltpu.roll(right, 127 - at, 1), pltpu.roll(tile, 127, 1)
            )
            for d, value in ((0, after), (1, tile), (2, before)):
                high[d, xp, :, (z + 1) * 128 : (z + 2) * 128], low[
                    d, xp, :, (z + 1) * 128 : (z + 2) * 128
                ] = split(value)


def taps(ref, x):
    return jnp.concatenate(
        [
            ref[d, x + 2 - a, :, (2 - b) * 128 : (2 - b) * 128 + 512]
            for a in range(3)
            for b in range(3)
            for d in range(3)
        ],
        axis=0,
    )


def x_row(ref, x):
    return jnp.concatenate([ref[pl.ds(x * 4 + z, CI, stride=16), :] for z in range(4)], axis=1)


def filter_kernel(
    chan, odd, core, own, other, grad, near_row, far_row, from_core, from_chip, out, high, low
):
    at_left = core[0] == 0
    left = jnp.where(at_left, from_chip[...], from_core[...])
    right = jnp.where(at_left, from_core[...], from_chip[...])
    spread(odd, grad, near_row, far_row, left, right, high, low)
    is_first = chan[0] == 0
    total = None
    for x in range(4):
        mine, theirs = x_row(own, x), x_row(other, x)
        act = jnp.concatenate(
            [jnp.where(is_first, mine, theirs), jnp.where(is_first, theirs, mine)], axis=0
        )
        act_high, act_low = split(act)
        both = jnp.concatenate([act_high, act_low], axis=0)
        p = lax.dot_general(taps(high, x), both, NT, preferred_element_type=F32)
        q = lax.dot_general(taps(low, x), act_high, NT, preferred_element_type=F32)
        part = p[:, :64] + p[:, 64:] + q
        total = part if total is None else total + part
    total = total * (1.0 / 512.0)
    for j in range(16):
        if j < 13:
            pair = [total[64 * j : 64 * j + 32], total[64 * j + 32 : 64 * j + 64]]
        elif j == 13:
            pair = [total[64 * j : 64 * j + 32], jnp.zeros((32, 64), F32)]
        else:
            pair = [jnp.zeros((32, 64), F32)] * 2
        out[32 * j : 32 * j + 32, :] = jnp.concatenate(pair, axis=1)


def data_kernel(chan, weights, high, low, kept, sent):
    w = weights[...].reshape(864, 64)
    w = jnp.where(chan[0] == 0, w, jnp.concatenate([w[:, 32:], w[:, :32]], axis=1))
    w_high = w.astype(BF16).astype(F32)
    both = jnp.concatenate([w_high, w - w_high], axis=1)
    both = jnp.concatenate([both, jnp.zeros((32, 128), F32)], axis=0)
    both = both.T.astype(BF16)[:, :864]
    for x in range(4):
        p = jnp.dot(both, taps(high, x), preferred_element_type=F32)
        q = jnp.dot(both[:64], taps(low, x), preferred_element_type=F32)
        result = p[:64] + p[64:] + q
        for z in range(4):
            tile = result[:, z * 128 : (z + 1) * 128]
            kept[pl.ds(x * 4 + z, CI, stride=16), :] = tile[:32]
            sent[pl.ds(x * 4 + z, CI, stride=16), :] = tile[32:]


def sum_kernel(copies, pieces, out):
    def run(values, result):
        total = values[0:32, :]
        for j in range(1, pieces):
            total = total + values[32 * j : 32 * j + 32, :]
        for j in range(copies):
            result[32 * j : 32 * j + 32, :] = total

    return run


def unpack_kernel(packed, out):
    for tap in range(27):
        half = 64 * (tap % 2)
        out[tap, :, :] = packed[32 * (tap // 2) : 32 * (tap // 2) + 32, half : half + 64]


VMEM = pl.BlockSpec(memory_space=pltpu.VMEM)
SMEM = pl.BlockSpec(memory_space=pltpu.SMEM)
PARAMS = pltpu.CompilerParams(vmem_limit_bytes=40 * 2**20)


def shape(*dims, dtype=F32):
    return jax.ShapeDtypeStruct(dims, dtype)


def call(kernel, outs, in_specs, flops=0, moved=0):
    return pl.pallas_call(
        kernel,
        out_shape=outs,
        in_specs=in_specs,
        out_specs=jax.tree.map(lambda _: VMEM, outs),
        compiler_params=PARAMS,
        cost_estimate=pl.CostEstimate(flops=flops, bytes_accessed=moved, transcendentals=0),
    )


def summed(values, copies):
    rows = values.shape[0]
    return call(sum_kernel(copies, rows // 32, None), shape(32 * copies, 128), [VMEM])(values)


def summed_over_tiles(partial):
    near, far = lax.axis_size(NEAR), lax.axis_size(FAR)
    pieces = lax.all_to_all(partial, NEAR, 0, 0, tiled=True)
    copies = lax.all_to_all(summed(pieces, far), FAR, 0, 0, tiled=True)
    return lax.all_to_all(summed(copies, near), NEAR, 0, 0, tiled=True)


def place(axis):
    return lax.axis_index(axis).astype(jnp.int32).reshape(1)


def body(activation, out_grad, kernel):
    act = activation.reshape(512, 128)
    grad = out_grad.reshape(512, 128)
    chan, odd, core = place("chan"), lax.rem(place("y"), 2), place("c")
    rows = grad.reshape(CI, 4, 4, 128)
    top, bottom = rows[:, 3].reshape(128, 128), rows[:, 0].reshape(128, 128)
    is_odd = odd[0] == 1
    near_row = swapped(jnp.where(is_odd, bottom, top), ALONG_X, 0)
    far_row = swapped(jnp.where(is_odd, top, bottom), ALONG_X, 1)
    other = swapped(act, "chan", 0)
    to_core, to_chip = call(edges_kernel, (shape(CI, 128),) * 2, [SMEM] * 2 + [VMEM] * 3)(
        odd, core, grad, near_row, far_row
    )
    from_core = swapped(to_core, "c", 0)
    from_chip = swapped(to_chip, ALONG_Y, 1)
    halves = shape(3, 6, CI, 768, dtype=BF16)
    partial, high, low = call(
        filter_kernel, (shape(512, 128), halves, halves), [SMEM] * 3 + [VMEM] * 7, 700_000_000, 1 << 22
    )(chan, odd, core, act, other, grad, near_row, far_row, from_core, from_chip)
    kept, sent = call(
        data_kernel, (shape(512, 128),) * 2, [SMEM] + [VMEM] * 3, 700_000_000, 1 << 22
    )(chan, kernel, high, low)
    input_grad = (kept + swapped(sent, "chan", 0)).reshape(activation.shape)
    packed = summed_over_tiles(partial)
    kernel_grad = call(unpack_kernel, shape(27, 32, 64), [VMEM])(packed)
    return (input_grad, kernel_grad)


def solution(mesh):
    mesh = Mesh(mesh.devices.reshape(8, 4, 2, 2, 2), TILE + ("chan",))
    field = P("chan", TILE, None, None, None)
    weights = P(None, "chan", None)
    return jax.shard_map(
        body,
        mesh=mesh,
        in_specs=(field, field, weights),
        out_specs=(field, weights),
        check_vma=False,
    )
```

```python
import jax
import jax.numpy as jnp
from jax import lax
from jax.experimental import pallas as pl
from jax.experimental.pallas import tpu as pltpu
from jax.sharding import Mesh, PartitionSpec as P

F32, BF16 = jnp.float32, jnp.bfloat16
ALONG_X = ("z", "y")
ALONG_Y = ("xh", "c")
TILE = ALONG_X + ALONG_Y
CI = 32
NT = (((1,), (1,)), ((), ()))


def swapped(value, axis, first):
    count = lax.axis_size(axis)
    pairs = [(s, (s + 1) % count) for s in range(first, count, 2)]
    return lax.ppermute(value, axis, pairs + [(t, s) for s, t in pairs])


def split(value):
    high = value.astype(BF16)
    return high, (value - high.astype(F32)).astype(BF16)


def rows_kernel(along, grad, near, far):
    odd = is_odd(along)
    for z in range(4):
        top = grad[pl.ds(12 + z, CI, stride=16), :]
        bottom = grad[pl.ds(z, CI, stride=16), :]
        near[pl.ds(z, CI, stride=4), :] = jnp.where(odd, bottom, top)
        far[pl.ds(z, CI, stride=4), :] = jnp.where(odd, top, bottom)


def edges_kernel(along, across, grad, near_row, far_row, to_core, to_chip):
    lane = lax.broadcasted_iota(jnp.int32, (CI, 128), 1)
    heads = jnp.zeros((CI, 128), F32)
    tails = jnp.zeros((CI, 128), F32)
    for xp in range(6):
        for z in range(4):
            tile = extended(along, grad, near_row, far_row, xp, z)
            at = 6 * xp + z + 1
            heads = jnp.where(lane == at, pltpu.roll(tile, at, 1), heads)
            tails = jnp.where(lane == at, pltpu.roll(tile, at + 1, 1), tails)
    odd = is_odd(across)
    to_core[...] = jnp.where(odd, heads, tails)
    to_chip[...] = jnp.where(odd, tails, heads)


def extended(along, grad, near_row, far_row, xp, z):
    if 0 < xp < 5:
        return grad[pl.ds((xp - 1) * 4 + z, CI, stride=16), :]
    near = near_row[pl.ds(z, CI, stride=4), :]
    far = far_row[pl.ds(z, CI, stride=4), :]
    row = jnp.where(is_odd(along) == (xp == 0), near, far)
    return jnp.where(along[0] == (0 if xp == 0 else 31), 0.0, row)


def is_odd(place):
    return (place[0] & 1) == 1


def spread(along, grad, near_row, far_row, left, right, high, low):
    lane = lax.broadcasted_iota(jnp.int32, (CI, 128), 1)
    zero = jnp.zeros((CI, 128), BF16)
    for xp in range(6):
        for d in range(3):
            for ref in (high, low):
                ref[d, xp, :, 0:128] = zero
                ref[d, xp, :, 640:768] = zero
        for z in range(4):
            tile = extended(along, grad, near_row, far_row, xp, z)
            before, after = pltpu.roll(tile, 1, 1), pltpu.roll(tile, 127, 1)
            if left is None:
                before = jnp.where(lane == 0, 0.0, before)
                after = jnp.where(lane == 127, 0.0, after)
            else:
                at = 6 * xp + z + 1
                before = jnp.where(lane == 0, pltpu.roll(left, 128 - at, 1), before)
                after = jnp.where(lane == 127, pltpu.roll(right, 127 - at, 1), after)
            for d, value in ((0, after), (1, tile), (2, before)):
                high[d, xp, :, (z + 1) * 128 : (z + 2) * 128], low[
                    d, xp, :, (z + 1) * 128 : (z + 2) * 128
                ] = split(value)


def taps(ref, x):
    return jnp.concatenate(
        [
            ref[d, x + 2 - a, :, (2 - b) * 128 : (2 - b) * 128 + 512]
            for a in range(3)
            for b in range(3)
            for d in range(3)
        ],
        axis=0,
    )


def x_row(ref, x):
    return jnp.concatenate([ref[pl.ds(x * 4 + z, CI, stride=16), :] for z in range(4)], axis=1)


def filter_kernel(
    chan, along, own, other, grad, near_row, far_row, total_out, first_out, last_out, high, low
):
    spread(along, grad, near_row, far_row, None, None, high, low)
    is_first = chan[0] == 0
    lane = lax.broadcasted_iota(jnp.int32, (64, 128), 1)
    heads = jnp.zeros((64, 128), F32)
    tails = jnp.zeros((64, 128), F32)
    total = None
    for x in range(4):
        mine, theirs = x_row(own, x), x_row(other, x)
        act = jnp.concatenate(
            [jnp.where(is_first, mine, theirs), jnp.where(is_first, theirs, mine)], axis=0
        )
        for z in range(4):
            at, tile = 6 * x + z, act[:, 128 * z : 128 * z + 128]
            heads = jnp.where(lane == at, pltpu.roll(tile, at, 1) if at else tile, heads)
            tails = jnp.where(lane == at, pltpu.roll(tile, at + 1, 1), tails)
        act_high, act_low = split(act)
        both = jnp.concatenate([act_high, act_low], axis=0)
        p = lax.dot_general(taps(high, x), both, NT, preferred_element_type=F32)
        q = lax.dot_general(taps(low, x), act_high, NT, preferred_element_type=F32)
        part = p[:, :64] + p[:, 64:] + q
        total = part if total is None else total + part
    total_out[...] = total
    first_out[...] = heads
    last_out[...] = tails


def rims(across, from_core, from_chip):
    odd = is_odd(across)
    left = jnp.where(odd, from_core[...], from_chip[...])
    right = jnp.where(odd, from_chip[...], from_core[...])
    return jnp.where(across[0] == 0, 0.0, left), jnp.where(across[0] == 3, 0.0, right)


def rim_taps(rim, column):
    shifted = jnp.concatenate(
        [
            pltpu.roll(rim, 128 - (6 * (2 - a) + 2 - b), 1) if a + b < 4 else rim
            for a in range(3)
            for b in range(3)
        ],
        axis=0,
    )
    high, low = split(shifted)
    col_high, col_low = split(column)
    both = jnp.concatenate([col_high, col_low], axis=0)
    p = lax.dot_general(high, both, NT, preferred_element_type=F32)
    q = lax.dot_general(low, col_high, NT, preferred_element_type=F32)
    return p[:, :64] + p[:, 64:] + q


def rim_kernel(across, total, first, last, from_core, from_chip, keep, give):
    left, right = rims(across, from_core, from_chip)
    extra = {2: rim_taps(left, first[...]), 0: rim_taps(right, last[...])}

    def of_tap(tap):
        if tap > 26:
            return jnp.zeros((CI, 64), F32)
        value = total[CI * tap : CI * tap + CI, :]
        group, d = divmod(tap, 3)
        if d in extra:
            value = value + extra[d][CI * group : CI * group + CI]
        return value * (1.0 / 512.0)

    odd = is_odd(across)
    for j in range(8):
        pairs = [
            jnp.concatenate([of_tap(2 * pair), of_tap(2 * pair + 1)], axis=1)
            for pair in (j, j + 8)
        ]
        keep[32 * j : 32 * j + 32, :] = jnp.where(odd, pairs[1], pairs[0])
        give[32 * j : 32 * j + 32, :] = jnp.where(odd, pairs[0], pairs[1])


def data_kernel(
    chan, along, across, weights, grad, near_row, far_row, from_core, from_chip, kept, sent, high, low
):
    left, right = rims(across, from_core, from_chip)
    spread(along, grad, near_row, far_row, left, right, high, low)
    w = weights[...].reshape(864, 64)
    w = jnp.where(chan[0] == 0, w, jnp.concatenate([w[:, 32:], w[:, :32]], axis=1))
    w_high = w.astype(BF16).astype(F32)
    both = jnp.concatenate([w_high, w - w_high], axis=1)
    both = jnp.concatenate([both, jnp.zeros((32, 128), F32)], axis=0)
    both = both.T.astype(BF16)[:, :864]
    for x in range(4):
        p = jnp.dot(both, taps(high, x), preferred_element_type=F32)
        q = jnp.dot(both[:64], taps(low, x), preferred_element_type=F32)
        result = p[:64] + p[64:] + q
        for z in range(4):
            tile = result[:, z * 128 : (z + 1) * 128]
            kept[pl.ds(x * 4 + z, CI, stride=16), :] = tile[:32]
            sent[pl.ds(x * 4 + z, CI, stride=16), :] = tile[32:]


def quarter(ref, index):
    return ref[pl.ds(pl.multiple_of(index * 64, 64), 64), :]


def quarters_kernel(row, kept, received, own, one, two, three, both):
    both[...] = kept[...] + received[...]
    for bits, out in enumerate((own, one, two, three)):
        out[...] = quarter(both, row[0] ^ bits)


def sum_kernel(own, one, two, three, out):
    out[...] = (own[...] + one[...]) + (two[...] + three[...])


def copies_kernel(own, other, out):
    total = own[...] + other[...]
    for j in range(8):
        out[64 * j : 64 * j + 64, :] = total


def fold_kernel(pieces, out):
    total = pieces[0:64, :]
    for j in range(1, 8):
        total = total + pieces[64 * j : 64 * j + 64, :]
    out[...] = total


def join_kernel(core, own, other, out):
    at_left = core[0] == 0
    out[0:64, :] = jnp.where(at_left, own[...], other[...])
    out[64:128, :] = jnp.where(at_left, other[...], own[...])


def unpack_kernel(row, own, one, two, three, out):
    low_bit, high_bit = (row[0] & 1) == 0, (row[0] & 2) == 0
    refs = (own, one, two, three)
    for part in range(4):
        a, b, c, d = (refs[part ^ bits][...] for bits in range(4))
        value = jnp.where(high_bit, jnp.where(low_bit, a, b), jnp.where(low_bit, c, d))
        for half in range(2):
            for j in range(2):
                pair = 8 * half + 2 * part + j
                rows = value[64 * half + 32 * j : 64 * half + 32 * j + 32]
                for k in range(2):
                    if 2 * pair + k < 27:
                        out[2 * pair + k, :, :] = rows[:, 64 * k : 64 * k + 64]


VMEM = pl.BlockSpec(memory_space=pltpu.VMEM)
SMEM = pl.BlockSpec(memory_space=pltpu.SMEM)
PARAMS = pltpu.CompilerParams(vmem_limit_bytes=40 * 2**20)


def shape(*dims, dtype=F32):
    return jax.ShapeDtypeStruct(dims, dtype)


def call(kernel, outs, in_specs, scratch=(), flops=0, moved=0):
    return pl.pallas_call(
        kernel,
        out_shape=outs,
        in_specs=in_specs,
        out_specs=jax.tree.map(lambda _: VMEM, outs),
        scratch_shapes=scratch,
        compiler_params=PARAMS,
        cost_estimate=pl.CostEstimate(flops=flops, bytes_accessed=moved, transcendentals=0),
    )


def crossed(value, bits):
    return lax.ppermute(value, "y", [(s, s ^ bits) for s in range(4)])


def summed_over_tiles(keep, give):
    row, core = place("y"), place("c")
    small = shape(64, 128)
    own, one, two, three = call(
        quarters_kernel, (small,) * 4, [SMEM, VMEM, VMEM], [pltpu.VMEM((256, 128), F32)]
    )(row, keep, swapped(give, "c", 0))
    two, one, three = crossed(two, 2), crossed(one, 1), crossed(three, 3)
    part = call(sum_kernel, small, [VMEM] * 4)(own, one, two, three)
    copies = call(copies_kernel, shape(512, 128), [VMEM] * 2)(part, swapped(part, "xh", 0))
    copies = lax.all_to_all(copies, "z", 0, 0, tiled=True)
    part = call(fold_kernel, small, [VMEM])(copies)
    part = call(join_kernel, shape(128, 128), [SMEM, VMEM, VMEM])(core, part, swapped(part, "c", 0))
    two, one, three = crossed(part, 2), crossed(part, 1), crossed(part, 3)
    return call(unpack_kernel, shape(27, 32, 64), [SMEM] + [VMEM] * 4)(row, part, one, two, three)


def place(axis):
    return lax.axis_index(axis).astype(jnp.int32).reshape(1)


def body(activation, out_grad, kernel):
    act = activation.reshape(512, 128)
    grad = out_grad.reshape(512, 128)
    chan, along, across = place("chan"), place(ALONG_X), place(ALONG_Y)
    other = swapped(act, "chan", 0)
    to_near, to_far = call(rows_kernel, (shape(128, 128),) * 2, [SMEM, VMEM])(along, grad)
    far_row = swapped(to_far, ALONG_X, 1)
    near_row = swapped(to_near, ALONG_X, 0)
    to_core, to_chip = call(edges_kernel, (shape(CI, 128),) * 2, [SMEM] * 2 + [VMEM] * 3)(
        along, across, grad, near_row, far_row
    )
    from_core = swapped(to_core, "c", 0)
    from_chip = swapped(to_chip, ALONG_Y, 1)
    halves = [pltpu.VMEM((3, 6, CI, 768), BF16)] * 2
    column = shape(64, 128)
    total, first, last = call(
        filter_kernel, (shape(864, 64), column, column), [SMEM] * 2 + [VMEM] * 5, halves, 700_000_000, 1 << 22
    )(chan, along, act, other, grad, near_row, far_row)
    keep, give = call(rim_kernel, (shape(256, 128),) * 2, [SMEM] + [VMEM] * 5)(
        across, total, first, last, from_core, from_chip
    )
    kept, sent = call(
        data_kernel, (shape(512, 128),) * 2, [SMEM] * 3 + [VMEM] * 6, halves, 700_000_000, 1 << 22
    )(chan, along, across, kernel, grad, near_row, far_row, from_core, from_chip)
    input_grad = (kept + swapped(sent, "chan", 0)).reshape(activation.shape)
    kernel_grad = summed_over_tiles(keep, give)
    return (input_grad, kernel_grad)


def solution(mesh):
    mesh = Mesh(mesh.devices.reshape(8, 4, 2, 2, 2), TILE + ("chan",))
    field = P("chan", TILE, None, None, None)
    weights = P(None, "chan", None)
    return jax.shard_map(
        body,
        mesh=mesh,
        in_specs=(field, field, weights),
        out_specs=(field, weights),
        check_vma=False,
    )
```

```python
import jax
import jax.numpy as jnp
from jax import lax
from jax.experimental import pallas as pl
from jax.experimental.pallas import tpu as pltpu
from jax.sharding import Mesh, PartitionSpec as P

F32, BF16 = jnp.float32, jnp.bfloat16
ALONG_X = ("z", "y")
ALONG_Y = ("xh", "c")
TILE = ALONG_X + ALONG_Y
CI = 32
NT = (((1,), (1,)), ((), ()))


def swapped(value, axis, first):
    count = lax.axis_size(axis)
    pairs = [(s, (s + 1) % count) for s in range(first, count, 2)]
    return lax.ppermute(value, axis, pairs + [(t, s) for s, t in pairs])


def split(value):
    high = value.astype(BF16)
    return high, (value - high.astype(F32)).astype(BF16)


def rows_kernel(along, grad, far, near):
    odd = is_odd(along)
    for z in range(4):
        top = grad[pl.ds(12 + z, CI, stride=16), :]
        bottom = grad[pl.ds(z, CI, stride=16), :]
        far[pl.ds(z, CI, stride=4), :] = jnp.where(odd, top, bottom)
        near[pl.ds(z, CI, stride=4), :] = jnp.where(odd, bottom, top)


def edges_kernel(along, across, grad, far_row, near_row, to_chip, to_core):
    lane = lax.broadcasted_iota(jnp.int32, (CI, 128), 1)
    heads = jnp.zeros((CI, 128), F32)
    tails = jnp.zeros((CI, 128), F32)
    for xp in range(6):
        for z in range(4):
            tile = extended(along, grad, far_row, near_row, xp, z)
            at = 6 * xp + z + 1
            heads = jnp.where(lane == at, pltpu.roll(tile, at, 1), heads)
            tails = jnp.where(lane == at, pltpu.roll(tile, at + 1, 1), tails)
    odd = is_odd(across)
    to_core[...] = jnp.where(odd, heads, tails)
    to_chip[...] = jnp.where(odd, tails, heads)


def extended(along, grad, far_row, near_row, xp, z):
    if 0 < xp < 5:
        return grad[pl.ds((xp - 1) * 4 + z, CI, stride=16), :]
    near = near_row[pl.ds(z, CI, stride=4), :]
    far = far_row[pl.ds(z, CI, stride=4), :]
    row = jnp.where(is_odd(along) == (xp == 0), near, far)
    return jnp.where(along[0] == (0 if xp == 0 else 31), 0.0, row)


def is_odd(place):
    return (place[0] & 1) == 1


def spread(along, grad, far_row, near_row, left, right, high, low):
    lane = lax.broadcasted_iota(jnp.int32, (CI, 128), 1)
    zero = jnp.zeros((CI, 128), BF16)
    for xp in range(6):
        for d in range(3):
            for ref in (high, low):
                ref[d, xp, :, 0:128] = zero
                ref[d, xp, :, 640:768] = zero
        for z in range(4):
            tile = extended(along, grad, far_row, near_row, xp, z)
            before, after = pltpu.roll(tile, 1, 1), pltpu.roll(tile, 127, 1)
            if left is None:
                before = jnp.where(lane == 0, 0.0, before)
                after = jnp.where(lane == 127, 0.0, after)
            else:
                at = 6 * xp + z + 1
                before = jnp.where(lane == 0, pltpu.roll(left, 128 - at, 1), before)
                after = jnp.where(lane == 127, pltpu.roll(right, 127 - at, 1), after)
            for d, value in ((0, after), (1, tile), (2, before)):
                high[d, xp, :, (z + 1) * 128 : (z + 2) * 128], low[
                    d, xp, :, (z + 1) * 128 : (z + 2) * 128
                ] = split(value)


def taps(ref, x):
    return jnp.concatenate(
        [
            ref[d, x + 2 - a, :, (2 - b) * 128 : (2 - b) * 128 + 512]
            for a in range(3)
            for b in range(3)
            for d in range(3)
        ],
        axis=0,
    )


def x_row(ref, x):
    return jnp.concatenate([ref[pl.ds(x * 4 + z, CI, stride=16), :] for z in range(4)], axis=1)


def filter_kernel(
    chan, along, own, other, grad, far_row, near_row, total_out, first_out, last_out, high, low
):
    spread(along, grad, far_row, near_row, None, None, high, low)
    is_first = chan[0] == 0
    lane = lax.broadcasted_iota(jnp.int32, (64, 128), 1)
    heads = jnp.zeros((64, 128), F32)
    tails = jnp.zeros((64, 128), F32)
    total = None
    for x in range(4):
        mine, theirs = x_row(own, x), x_row(other, x)
        act = jnp.concatenate(
            [jnp.where(is_first, mine, theirs), jnp.where(is_first, theirs, mine)], axis=0
        )
        for z in range(4):
            at, tile = 6 * x + z, act[:, 128 * z : 128 * z + 128]
            heads = jnp.where(lane == at, pltpu.roll(tile, at, 1) if at else tile, heads)
            tails = jnp.where(lane == at, pltpu.roll(tile, at + 1, 1), tails)
        act_high, act_low = split(act)
        both = jnp.concatenate([act_high, act_low], axis=0)
        p = lax.dot_general(taps(high, x), both, NT, preferred_element_type=F32)
        q = lax.dot_general(taps(low, x), act_high, NT, preferred_element_type=F32)
        part = p[:, :64] + p[:, 64:] + q
        total = part if total is None else total + part
    total_out[...] = total
    first_out[...] = heads
    last_out[...] = tails


def rims(across, from_chip, from_core):
    odd = is_odd(across)
    left = jnp.where(odd, from_core[...], from_chip[...])
    right = jnp.where(odd, from_chip[...], from_core[...])
    return jnp.where(across[0] == 0, 0.0, left), jnp.where(across[0] == 3, 0.0, right)


def rim_taps(rim, column):
    shifted = jnp.concatenate(
        [
            pltpu.roll(rim, 128 - (6 * (2 - a) + 2 - b), 1) if a + b < 4 else rim
            for a in range(3)
            for b in range(3)
        ],
        axis=0,
    )
    high, low = split(shifted)
    col_high, col_low = split(column)
    both = jnp.concatenate([col_high, col_low], axis=0)
    p = lax.dot_general(high, both, NT, preferred_element_type=F32)
    q = lax.dot_general(low, col_high, NT, preferred_element_type=F32)
    return p[:, :64] + p[:, 64:] + q


def rim_kernel(across, total, first, last, from_chip, from_core, keep, give):
    left, right = rims(across, from_chip, from_core)
    extra = {2: rim_taps(left, first[...]), 0: rim_taps(right, last[...])}

    def of_tap(tap):
        if tap > 26:
            return jnp.zeros((CI, 64), F32)
        value = total[CI * tap : CI * tap + CI, :]
        group, d = divmod(tap, 3)
        if d in extra:
            value = value + extra[d][CI * group : CI * group + CI]
        return value * (1.0 / 512.0)

    odd = is_odd(across)
    for j in range(7):
        pairs = [
            jnp.concatenate([of_tap(2 * pair), of_tap(2 * pair + 1)], axis=1)
            for pair in (j, j + 7)
        ]
        keep[32 * j : 32 * j + 32, :] = jnp.where(odd, pairs[1], pairs[0])
        give[32 * j : 32 * j + 32, :] = jnp.where(odd, pairs[0], pairs[1])


def data_kernel(
    chan, along, across, weights, grad, far_row, near_row, from_chip, from_core, kept, sent, high, low
):
    left, right = rims(across, from_chip, from_core)
    spread(along, grad, far_row, near_row, left, right, high, low)
    w = weights[...].reshape(864, 64)
    w = jnp.where(chan[0] == 0, w, jnp.concatenate([w[:, 32:], w[:, :32]], axis=1))
    w_high = w.astype(BF16).astype(F32)
    both = jnp.concatenate([w_high, w - w_high], axis=1)
    both = jnp.concatenate([both, jnp.zeros((32, 128), F32)], axis=0)
    both = both.T.astype(BF16)[:, :864]
    for x in range(4):
        p = jnp.dot(both, taps(high, x), preferred_element_type=F32)
        q = jnp.dot(both[:64], taps(low, x), preferred_element_type=F32)
        result = p[:64] + p[64:] + q
        for z in range(4):
            tile = result[:, z * 128 : (z + 1) * 128]
            kept[pl.ds(x * 4 + z, CI, stride=16), :] = tile[:32]
            sent[pl.ds(x * 4 + z, CI, stride=16), :] = tile[32:]


def quarter(ref, index):
    return ref[pl.ds(pl.multiple_of(index * 56, 8), 56), :]


def quarters_kernel(row, kept, received, own, one, two, three, both):
    both[...] = kept[...] + received[...]
    for bits, out in enumerate((own, one, two, three)):
        out[...] = quarter(both, row[0] ^ bits)


def sum_kernel(two, one, three, own, out):
    out[...] = (own[...] + one[...]) + (two[...] + three[...])


def copies_kernel(own, other, out):
    total = own[...] + other[...]
    for j in range(8):
        out[56 * j : 56 * j + 56, :] = total


def fold_kernel(pieces, out):
    total = pieces[0:56, :]
    for j in range(1, 8):
        total = total + pieces[56 * j : 56 * j + 56, :]
    out[...] = total


def join_kernel(row, two, one, three, own, out):
    low_bit, high_bit = (row[0] & 1) == 0, (row[0] & 2) == 0
    refs = (own, one, two, three)
    for part in range(4):
        a, b, c, d = (refs[part ^ bits][...] for bits in range(4))
        out[56 * part : 56 * part + 56, :] = jnp.where(
            high_bit, jnp.where(low_bit, a, b), jnp.where(low_bit, c, d)
        )


def unpack_kernel(core, own, other, out):
    odd = is_odd(core)
    for j in range(7):
        rows = slice(32 * j, 32 * j + 32)
        halves = (
            jnp.where(odd, other[rows, :], own[rows, :]),
            jnp.where(odd, own[rows, :], other[rows, :]),
        )
        for half in range(2):
            for k in range(2):
                tap = 14 * half + 2 * j + k
                if tap < 27:
                    out[tap, :, :] = halves[half][:, 64 * k : 64 * k + 64]


VMEM = pl.BlockSpec(memory_space=pltpu.VMEM)
SMEM = pl.BlockSpec(memory_space=pltpu.SMEM)
PARAMS = pltpu.CompilerParams(vmem_limit_bytes=40 * 2**20)


def shape(*dims, dtype=F32):
    return jax.ShapeDtypeStruct(dims, dtype)


def call(kernel, outs, in_specs, scratch=(), flops=0, moved=0):
    return pl.pallas_call(
        kernel,
        out_shape=outs,
        in_specs=in_specs,
        out_specs=jax.tree.map(lambda _: VMEM, outs),
        scratch_shapes=scratch,
        compiler_params=PARAMS,
        cost_estimate=pl.CostEstimate(flops=flops, bytes_accessed=moved, transcendentals=0),
    )


def crossed(value, axis, bits):
    return lax.ppermute(value, axis, [(s, s ^ bits) for s in range(lax.axis_size(axis))])


def summed_over_tiles(keep, give):
    row, core = place("y"), place("c")
    small = shape(56, 128)
    own, one, two, three = call(
        quarters_kernel, (small,) * 4, [SMEM, VMEM, VMEM], [pltpu.VMEM((224, 128), F32)]
    )(row, keep, swapped(give, "c", 0))
    two, one, three = (crossed(v, "y", bits) for v, bits in ((two, 2), (one, 1), (three, 3)))
    part = call(sum_kernel, small, [VMEM] * 4)(two, one, three, own)
    copies = call(copies_kernel, shape(448, 128), [VMEM] * 2)(part, swapped(part, "xh", 0))
    part = call(fold_kernel, small, [VMEM])(lax.all_to_all(copies, "z", 0, 0, tiled=True))
    two, one, three = (crossed(part, "y", bits) for bits in (2, 1, 3))
    half = call(join_kernel, shape(224, 128), [SMEM] + [VMEM] * 4)(row, two, one, three, part)
    return call(unpack_kernel, shape(27, 32, 64), [SMEM, VMEM, VMEM])(
        core, half, swapped(half, "c", 0)
    )


def place(axis):
    return lax.axis_index(axis).astype(jnp.int32).reshape(1)


def body(activation, out_grad, kernel):
    act = activation.reshape(512, 128)
    grad = out_grad.reshape(512, 128)
    chan, along, across = place("chan"), place(ALONG_X), place(ALONG_Y)
    to_far, to_near = call(rows_kernel, (shape(128, 128),) * 2, [SMEM, VMEM])(along, grad)
    far_row = swapped(to_far, ALONG_X, 1)
    other = swapped(act, "chan", 0)
    near_row = swapped(to_near, ALONG_X, 0)
    to_chip, to_core = call(edges_kernel, (shape(CI, 128),) * 2, [SMEM] * 2 + [VMEM] * 3)(
        along, across, grad, far_row, near_row
    )
    from_chip = swapped(to_chip, ALONG_Y, 1)
    from_core = swapped(to_core, "c", 0)
    halves = [pltpu.VMEM((3, 6, CI, 768), BF16)] * 2
    column = shape(64, 128)
    total, first, last = call(
        filter_kernel, (shape(864, 64), column, column), [SMEM] * 2 + [VMEM] * 5, halves, 700_000_000, 1 << 22
    )(chan, along, act, other, grad, far_row, near_row)
    keep, give = call(rim_kernel, (shape(224, 128),) * 2, [SMEM] + [VMEM] * 5)(
        across, total, first, last, from_chip, from_core
    )
    kept, sent = call(
        data_kernel, (shape(512, 128),) * 2, [SMEM] * 3 + [VMEM] * 6, halves, 700_000_000, 1 << 22
    )(chan, along, across, kernel, grad, far_row, near_row, from_chip, from_core)
    input_grad = (kept + swapped(sent, "chan", 0)).reshape(activation.shape)
    kernel_grad = summed_over_tiles(keep, give)
    return (input_grad, kernel_grad)


def solution(mesh):
    mesh = Mesh(mesh.devices.reshape(8, 4, 2, 2, 2), TILE + ("chan",))
    field = P("chan", TILE, None, None, None)
    weights = P(None, "chan", None)
    return jax.shard_map(
        body,
        mesh=mesh,
        in_specs=(field, field, weights),
        out_specs=(field, weights),
        check_vma=False,
    )
```

```python
import jax
import jax.numpy as jnp
from jax import lax
from jax.experimental import pallas as pl
from jax.experimental.pallas import tpu as pltpu
from jax.sharding import Mesh, PartitionSpec as P

F32, BF16 = jnp.float32, jnp.bfloat16
ALONG_X = ("z", "y")
ALONG_Y = ("xh", "c")
TILE = ALONG_X + ALONG_Y
CI = 32
NT = (((1,), (1,)), ((), ()))


def swapped(value, axis, first):
    count = lax.axis_size(axis)
    pairs = [(s, (s + 1) % count) for s in range(first, count, 2)]
    return lax.ppermute(value, axis, pairs + [(t, s) for s, t in pairs])


def split(value):
    high = value.astype(BF16)
    return high, (value - high.astype(F32)).astype(BF16)


def rows_kernel(along, grad, far, near):
    odd = is_odd(along)
    for z in range(4):
        top = grad[pl.ds(12 + z, CI, stride=16), :]
        bottom = grad[pl.ds(z, CI, stride=16), :]
        far[pl.ds(z, CI, stride=4), :] = jnp.where(odd, top, bottom)
        near[pl.ds(z, CI, stride=4), :] = jnp.where(odd, bottom, top)


def edges_kernel(along, across, grad, far_row, near_row, to_chip, to_core):
    lane = lax.broadcasted_iota(jnp.int32, (CI, 128), 1)
    heads = jnp.zeros((CI, 128), F32)
    tails = jnp.zeros((CI, 128), F32)
    for xp in range(6):
        for z in range(4):
            tile = extended(along, grad, far_row, near_row, xp, z)
            at = 6 * xp + z + 1
            heads = jnp.where(lane == at, pltpu.roll(tile, at, 1), heads)
            tails = jnp.where(lane == at, pltpu.roll(tile, at + 1, 1), tails)
    odd = is_odd(across)
    to_core[...] = jnp.where(odd, heads, tails)
    to_chip[...] = jnp.where(odd, tails, heads)


def extended(along, grad, far_row, near_row, xp, z):
    if 0 < xp < 5:
        return grad[pl.ds((xp - 1) * 4 + z, CI, stride=16), :]
    near = near_row[pl.ds(z, CI, stride=4), :]
    far = far_row[pl.ds(z, CI, stride=4), :]
    row = jnp.where(is_odd(along) == (xp == 0), near, far)
    return jnp.where(along[0] == (0 if xp == 0 else 31), 0.0, row)


def is_odd(place):
    return (place[0] & 1) == 1


def spread(along, grad, far_row, near_row, left, right, high, low):
    lane = lax.broadcasted_iota(jnp.int32, (CI, 128), 1)
    zero = jnp.zeros((CI, 128), BF16)
    for xp in range(6):
        for d in range(3):
            for ref in (high, low):
                ref[d, xp, :, 0:128] = zero
                ref[d, xp, :, 640:768] = zero
        for z in range(4):
            tile = extended(along, grad, far_row, near_row, xp, z)
            before, after = pltpu.roll(tile, 1, 1), pltpu.roll(tile, 127, 1)
            if left is None:
                before = jnp.where(lane == 0, 0.0, before)
                after = jnp.where(lane == 127, 0.0, after)
            else:
                at = 6 * xp + z + 1
                before = jnp.where(lane == 0, pltpu.roll(left, 128 - at, 1), before)
                after = jnp.where(lane == 127, pltpu.roll(right, 127 - at, 1), after)
            for d, value in ((0, after), (1, tile), (2, before)):
                high[d, xp, :, (z + 1) * 128 : (z + 2) * 128], low[
                    d, xp, :, (z + 1) * 128 : (z + 2) * 128
                ] = split(value)


def taps(ref, x):
    return jnp.concatenate(
        [
            ref[d, x + 2 - a, :, (2 - b) * 128 : (2 - b) * 128 + 512]
            for a in range(3)
            for b in range(3)
            for d in range(3)
        ],
        axis=0,
    )


def x_row(ref, x):
    return jnp.concatenate([ref[pl.ds(x * 4 + z, CI, stride=16), :] for z in range(4)], axis=1)


def filter_kernel(
    chan, along, own, other, grad, far_row, near_row, total_out, first_out, last_out, high, low
):
    spread(along, grad, far_row, near_row, None, None, high, low)
    is_first = chan[0] == 0
    lane = lax.broadcasted_iota(jnp.int32, (64, 128), 1)
    heads = jnp.zeros((64, 128), F32)
    tails = jnp.zeros((64, 128), F32)
    total = None
    for x in range(4):
        mine, theirs = x_row(own, x), x_row(other, x)
        act = jnp.concatenate(
            [jnp.where(is_first, mine, theirs), jnp.where(is_first, theirs, mine)], axis=0
        )
        for z in range(4):
            at, tile = 6 * x + z, act[:, 128 * z : 128 * z + 128]
            heads = jnp.where(lane == at, pltpu.roll(tile, at, 1) if at else tile, heads)
            tails = jnp.where(lane == at, pltpu.roll(tile, at + 1, 1), tails)
        act_high, act_low = split(act)
        both = jnp.concatenate([act_high, act_low], axis=0)
        p = lax.dot_general(taps(high, x), both, NT, preferred_element_type=F32)
        q = lax.dot_general(taps(low, x), act_high, NT, preferred_element_type=F32)
        part = p[:, :64] + p[:, 64:] + q
        total = part if total is None else total + part
    total_out[...] = total
    first_out[...] = heads
    last_out[...] = tails


def rims(across, from_chip, from_core):
    odd = is_odd(across)
    left = jnp.where(odd, from_core[...], from_chip[...])
    right = jnp.where(odd, from_chip[...], from_core[...])
    return jnp.where(across[0] == 0, 0.0, left), jnp.where(across[0] == 3, 0.0, right)


def rim_taps(rim, column):
    shifted = jnp.concatenate(
        [
            pltpu.roll(rim, 128 - (6 * (2 - a) + 2 - b), 1) if a + b < 4 else rim
            for a in range(3)
            for b in range(3)
        ],
        axis=0,
    )
    high, low = split(shifted)
    col_high, col_low = split(column)
    both = jnp.concatenate([col_high, col_low], axis=0)
    p = lax.dot_general(high, both, NT, preferred_element_type=F32)
    q = lax.dot_general(low, col_high, NT, preferred_element_type=F32)
    return p[:, :64] + p[:, 64:] + q


def rim_kernel(across, total, first, last, from_chip, from_core, keep, give):
    left, right = rims(across, from_chip, from_core)
    extra = {2: rim_taps(left, first[...]), 0: rim_taps(right, last[...])}

    def of_tap(tap):
        if tap > 26:
            return jnp.zeros((CI, 64), F32)
        value = total[CI * tap : CI * tap + CI, :]
        group, d = divmod(tap, 3)
        if d in extra:
            value = value + extra[d][CI * group : CI * group + CI]
        return value * (1.0 / 512.0)

    odd = is_odd(across)
    for j in range(7):
        pairs = [
            jnp.concatenate([of_tap(2 * pair), of_tap(2 * pair + 1)], axis=1)
            for pair in (j, j + 7)
        ]
        keep[32 * j : 32 * j + 32, :] = jnp.where(odd, pairs[1], pairs[0])
        give[32 * j : 32 * j + 32, :] = jnp.where(odd, pairs[0], pairs[1])


def data_kernel(
    chan, along, across, after, weights, grad, far_row, near_row, from_chip, from_core, kept, sent, high, low
):
    left, right = rims(across, from_chip, from_core)
    spread(along, grad, far_row, near_row, left, right, high, low)
    w = weights[...].reshape(864, 64)
    w = jnp.where(chan[0] == 0, w, jnp.concatenate([w[:, 32:], w[:, :32]], axis=1))
    w_high = w.astype(BF16).astype(F32)
    both = jnp.concatenate([w_high, w - w_high], axis=1)
    both = jnp.concatenate([both, jnp.zeros((32, 128), F32)], axis=0)
    both = both.T.astype(BF16)[:, :864]
    for x in range(4):
        p = jnp.dot(both, taps(high, x), preferred_element_type=F32)
        q = jnp.dot(both[:64], taps(low, x), preferred_element_type=F32)
        result = p[:64] + p[64:] + q
        for z in range(4):
            tile = result[:, z * 128 : (z + 1) * 128]
            kept[pl.ds(x * 4 + z, CI, stride=16), :] = tile[:32]
            sent[pl.ds(x * 4 + z, CI, stride=16), :] = tile[32:]


def gate_kernel(value, after, out):
    out[...] = value[...]


def quarter(ref, index):
    return ref[pl.ds(pl.multiple_of(index * 56, 8), 56), :]


def quarters_kernel(row, kept, received, own, one, two, three, both):
    both[...] = kept[...] + received[...]
    for bits, out in enumerate((own, one, two, three)):
        out[...] = quarter(both, row[0] ^ bits)


def sum_kernel(two, three, one, own, out):
    out[...] = (own[...] + one[...]) + (two[...] + three[...])


def join_kernel(row, two, three, one, own, out):
    low_bit, high_bit = (row[0] & 1) == 0, (row[0] & 2) == 0
    refs = (own, one, two, three)
    for part in range(4):
        a, b, c, d = (refs[part ^ bits][...] for bits in range(4))
        out[56 * part : 56 * part + 56, :] = jnp.where(
            high_bit, jnp.where(low_bit, a, b), jnp.where(low_bit, c, d)
        )


def add_kernel(one, two, out, done):
    out[...] = one[...] + two[...]
    done[...] = one[0:8, :]


def unpack_kernel(core, own, other, after, out):
    odd = is_odd(core)
    for j in range(7):
        rows = slice(32 * j, 32 * j + 32)
        halves = (
            jnp.where(odd, other[rows, :], own[rows, :]),
            jnp.where(odd, own[rows, :], other[rows, :]),
        )
        for half in range(2):
            for k in range(2):
                tap = 14 * half + 2 * j + k
                if tap < 27:
                    out[tap, :, :] = halves[half][:, 64 * k : 64 * k + 64]


VMEM = pl.BlockSpec(memory_space=pltpu.VMEM)
SMEM = pl.BlockSpec(memory_space=pltpu.SMEM)
PARAMS = pltpu.CompilerParams(vmem_limit_bytes=40 * 2**20)


def shape(*dims, dtype=F32):
    return jax.ShapeDtypeStruct(dims, dtype)


def call(kernel, outs, in_specs, scratch=(), flops=0, moved=0):
    return pl.pallas_call(
        kernel,
        out_shape=outs,
        in_specs=in_specs,
        out_specs=jax.tree.map(lambda _: VMEM, outs),
        scratch_shapes=scratch,
        compiler_params=PARAMS,
        cost_estimate=pl.CostEstimate(flops=flops, bytes_accessed=moved, transcendentals=0),
    )


def crossed(value, axis, bits):
    return lax.ppermute(value, axis, [(s, s ^ bits) for s in range(lax.axis_size(axis))])


def summed_near(keep, give):
    row = place("y")
    small = shape(56, 128)
    own, one, two, three = call(
        quarters_kernel, (small,) * 4, [SMEM, VMEM, VMEM], [pltpu.VMEM((224, 128), F32)]
    )(row, keep, swapped(give, "c", 0))
    two, three, one = (crossed(v, "y", bits) for v, bits in ((two, 2), (three, 3), (one, 1)))
    return call(sum_kernel, small, [VMEM] * 4)(two, three, one, own)


def summed_far(part):
    part = part + swapped(part, "xh", 0)
    parts = [crossed(part, "z", bits) for bits in (3, 2, 1)]
    part = call(sum_kernel, shape(56, 128), [VMEM] * 4)(*parts, part)
    return part + crossed(part, "z", 6)


def gathered(part, done):
    row, core = place("y"), place("c")
    two, three, one = (crossed(part, "y", bits) for bits in (2, 3, 1))
    half = call(join_kernel, shape(224, 128), [SMEM] + [VMEM] * 4)(row, two, three, one, part)
    return call(unpack_kernel, shape(27, 32, 64), [SMEM, VMEM, VMEM, VMEM])(
        core, half, swapped(half, "c", 0), done
    )


def place(axis):
    return lax.axis_index(axis).astype(jnp.int32).reshape(1)


def body(activation, out_grad, kernel):
    act = activation.reshape(512, 128)
    grad = out_grad.reshape(512, 128)
    chan, along, across = place("chan"), place(ALONG_X), place(ALONG_Y)
    to_far, to_near = call(rows_kernel, (shape(128, 128),) * 2, [SMEM, VMEM])(along, grad)
    far_row = swapped(to_far, ALONG_X, 1)
    other = swapped(act, "chan", 0)
    near_row = swapped(to_near, ALONG_X, 0)
    to_chip, to_core = call(edges_kernel, (shape(CI, 128),) * 2, [SMEM] * 2 + [VMEM] * 3)(
        along, across, grad, far_row, near_row
    )
    from_chip = swapped(to_chip, ALONG_Y, 1)
    from_core = swapped(to_core, "c", 0)
    halves = [pltpu.VMEM((3, 6, CI, 768), BF16)] * 2
    column = shape(64, 128)
    total, first, last = call(
        filter_kernel, (shape(864, 64), column, column), [SMEM] * 2 + [VMEM] * 5, halves, 700_000_000, 1 << 22
    )(chan, along, act, other, grad, far_row, near_row)
    keep, give = call(rim_kernel, (shape(224, 128),) * 2, [SMEM] + [VMEM] * 5)(
        across, total, first, last, from_chip, from_core
    )
    part = summed_near(keep, give)
    kept, sent = call(
        data_kernel, (shape(512, 128),) * 2, [SMEM] * 3 + [VMEM] * 7, halves, 700_000_000, 1 << 22
    )(chan, along, across, part, kernel, grad, far_row, near_row, from_chip, from_core)
    part = summed_far(part)
    sent = call(gate_kernel, shape(512, 128), [VMEM] * 2)(sent, part)
    input_grad, done = call(add_kernel, (shape(512, 128), shape(8, 128)), [VMEM] * 2)(
        kept, swapped(sent, "chan", 0)
    )
    input_grad = input_grad.reshape(activation.shape)
    kernel_grad = gathered(part, done)
    return (input_grad, kernel_grad)


def solution(mesh):
    mesh = Mesh(mesh.devices.reshape(8, 4, 2, 2, 2), TILE + ("chan",))
    field = P("chan", TILE, None, None, None)
    weights = P(None, "chan", None)
    return jax.shard_map(
        body,
        mesh=mesh,
        in_specs=(field, field, weights),
        out_specs=(field, weights),
        check_vma=False,
    )
```

```python
import jax
import jax.numpy as jnp
from jax import lax
from jax.experimental import pallas as pl
from jax.experimental.pallas import tpu as pltpu
from jax.sharding import Mesh, PartitionSpec as P

F32, BF16 = jnp.float32, jnp.bfloat16
ALONG_X = ("z", "y")
ALONG_Y = ("xh", "c")
TILE = ALONG_X + ALONG_Y
CI = 32
NT = (((1,), (1,)), ((), ()))


def swapped(value, axis, first):
    count = lax.axis_size(axis)
    pairs = [(s, (s + 1) % count) for s in range(first, count, 2)]
    return lax.ppermute(value, axis, pairs + [(t, s) for s, t in pairs])


def split(value):
    high = value.astype(BF16)
    return high, (value - high.astype(F32)).astype(BF16)


def rows_kernel(along, grad, far, near):
    odd = is_odd(along)
    for z in range(4):
        top = grad[pl.ds(12 + z, CI, stride=16), :]
        bottom = grad[pl.ds(z, CI, stride=16), :]
        far[pl.ds(z, CI, stride=4), :] = jnp.where(odd, top, bottom)
        near[pl.ds(z, CI, stride=4), :] = jnp.where(odd, bottom, top)


def edges_kernel(along, across, grad, far_row, near_row, to_chip, to_core):
    lane = lax.broadcasted_iota(jnp.int32, (CI, 128), 1)
    heads = jnp.zeros((CI, 128), F32)
    tails = jnp.zeros((CI, 128), F32)
    for xp in range(6):
        for z in range(4):
            tile = extended(along, grad, far_row, near_row, xp, z)
            at = 6 * xp + z + 1
            heads = jnp.where(lane == at, pltpu.roll(tile, at, 1), heads)
            tails = jnp.where(lane == at, pltpu.roll(tile, at + 1, 1), tails)
    odd = is_odd(across)
    to_core[...] = jnp.where(odd, heads, tails)
    to_chip[...] = jnp.where(odd, tails, heads)


def extended(along, grad, far_row, near_row, xp, z):
    if 0 < xp < 5:
        return grad[pl.ds((xp - 1) * 4 + z, CI, stride=16), :]
    near = near_row[pl.ds(z, CI, stride=4), :]
    far = far_row[pl.ds(z, CI, stride=4), :]
    row = jnp.where(is_odd(along) == (xp == 0), near, far)
    return jnp.where(along[0] == (0 if xp == 0 else 31), 0.0, row)


def is_odd(place):
    return (place[0] & 1) == 1


def spread(along, grad, far_row, near_row, left, right, high, low):
    lane = lax.broadcasted_iota(jnp.int32, (CI, 128), 1)
    zero = jnp.zeros((CI, 128), BF16)
    for xp in range(6):
        for d in range(3):
            for ref in (high, low):
                ref[d, xp, :, 0:128] = zero
                ref[d, xp, :, 640:768] = zero
        for z in range(4):
            tile = extended(along, grad, far_row, near_row, xp, z)
            before, after = pltpu.roll(tile, 1, 1), pltpu.roll(tile, 127, 1)
            if left is None:
                before = jnp.where(lane == 0, 0.0, before)
                after = jnp.where(lane == 127, 0.0, after)
            else:
                at = 6 * xp + z + 1
                before = jnp.where(lane == 0, pltpu.roll(left, 128 - at, 1), before)
                after = jnp.where(lane == 127, pltpu.roll(right, 127 - at, 1), after)
            for d, value in ((0, after), (1, tile), (2, before)):
                high[d, xp, :, (z + 1) * 128 : (z + 2) * 128], low[
                    d, xp, :, (z + 1) * 128 : (z + 2) * 128
                ] = split(value)


def taps(ref, x):
    return jnp.concatenate(
        [
            ref[d, x + 2 - a, :, (2 - b) * 128 : (2 - b) * 128 + 512]
            for a in range(3)
            for b in range(3)
            for d in range(3)
        ],
        axis=0,
    )


def x_row(ref, x):
    return jnp.concatenate([ref[pl.ds(x * 4 + z, CI, stride=16), :] for z in range(4)], axis=1)


def filter_kernel(
    chan, along, own, other, grad, far_row, near_row, total_out, first_out, last_out, high, low
):
    spread(along, grad, far_row, near_row, None, None, high, low)
    is_first = chan[0] == 0
    lane = lax.broadcasted_iota(jnp.int32, (64, 128), 1)
    heads = jnp.zeros((64, 128), F32)
    tails = jnp.zeros((64, 128), F32)
    total = None
    for x in range(4):
        mine, theirs = x_row(own, x), x_row(other, x)
        act = jnp.concatenate(
            [jnp.where(is_first, mine, theirs), jnp.where(is_first, theirs, mine)], axis=0
        )
        for z in range(4):
            at, tile = 6 * x + z, act[:, 128 * z : 128 * z + 128]
            heads = jnp.where(lane == at, pltpu.roll(tile, at, 1) if at else tile, heads)
            tails = jnp.where(lane == at, pltpu.roll(tile, at + 1, 1), tails)
        act_high, act_low = split(act)
        both = jnp.concatenate([act_high, act_low], axis=0)
        p = lax.dot_general(taps(high, x), both, NT, preferred_element_type=F32)
        q = lax.dot_general(taps(low, x), act_high, NT, preferred_element_type=F32)
        part = p[:, :64] + p[:, 64:] + q
        total = part if total is None else total + part
    total_out[...] = total
    first_out[...] = heads
    last_out[...] = tails


def rims(across, from_chip, from_core):
    odd = is_odd(across)
    left = jnp.where(odd, from_core[...], from_chip[...])
    right = jnp.where(odd, from_chip[...], from_core[...])
    return jnp.where(across[0] == 0, 0.0, left), jnp.where(across[0] == 3, 0.0, right)


def rim_taps(rim, column):
    shifted = jnp.concatenate(
        [
            pltpu.roll(rim, 128 - (6 * (2 - a) + 2 - b), 1) if a + b < 4 else rim
            for a in range(3)
            for b in range(3)
        ],
        axis=0,
    )
    high, low = split(shifted)
    col_high, col_low = split(column)
    both = jnp.concatenate([col_high, col_low], axis=0)
    p = lax.dot_general(high, both, NT, preferred_element_type=F32)
    q = lax.dot_general(low, col_high, NT, preferred_element_type=F32)
    return p[:, :64] + p[:, 64:] + q


def rim_kernel(across, total, first, last, from_chip, from_core, keep, give):
    left, right = rims(across, from_chip, from_core)
    extra = {2: rim_taps(left, first[...]), 0: rim_taps(right, last[...])}

    def of_tap(tap):
        if tap > 26:
            return jnp.zeros((CI, 64), F32)
        value = total[CI * tap : CI * tap + CI, :]
        group, d = divmod(tap, 3)
        if d in extra:
            value = value + extra[d][CI * group : CI * group + CI]
        return value * (1.0 / 512.0)

    odd = is_odd(across)
    for j in range(7):
        pairs = [
            jnp.concatenate([of_tap(2 * pair), of_tap(2 * pair + 1)], axis=1)
            for pair in (j, j + 7)
        ]
        keep[32 * j : 32 * j + 32, :] = jnp.where(odd, pairs[1], pairs[0])
        give[32 * j : 32 * j + 32, :] = jnp.where(odd, pairs[0], pairs[1])


def data_kernel(
    chan, along, across, after, weights, grad, far_row, near_row, from_chip, from_core, kept, sent, high, low
):
    left, right = rims(across, from_chip, from_core)
    spread(along, grad, far_row, near_row, left, right, high, low)
    w = weights[...].reshape(864, 64)
    w = jnp.where(chan[0] == 0, w, jnp.concatenate([w[:, 32:], w[:, :32]], axis=1))
    w_high = w.astype(BF16).astype(F32)
    both = jnp.concatenate([w_high, w - w_high], axis=1)
    both = jnp.concatenate([both, jnp.zeros((32, 128), F32)], axis=0)
    both = both.T.astype(BF16)[:, :864]
    for x in range(4):
        p = jnp.dot(both, taps(high, x), preferred_element_type=F32)
        q = jnp.dot(both[:64], taps(low, x), preferred_element_type=F32)
        result = p[:64] + p[64:] + q
        for z in range(4):
            tile = result[:, z * 128 : (z + 1) * 128]
            kept[pl.ds(x * 4 + z, CI, stride=16), :] = tile[:32]
            sent[pl.ds(x * 4 + z, CI, stride=16), :] = tile[32:]


def gate_kernel(value, after, out):
    out[...] = value[...]


def quarter(ref, index):
    return ref[pl.ds(pl.multiple_of(index * 56, 8), 56), :]


def quarters_kernel(row, kept, received, own, one, two, three, both):
    both[...] = kept[...] + received[...]
    for bits, out in enumerate((own, one, two, three)):
        out[...] = quarter(both, row[0] ^ bits)


def sum_kernel(three, two, one, own, out):
    out[...] = (own[...] + one[...]) + (two[...] + three[...])


def join_kernel(row, three, two, one, own, out):
    low_bit, high_bit = (row[0] & 1) == 0, (row[0] & 2) == 0
    refs = (own, one, two, three)
    for part in range(4):
        a, b, c, d = (refs[part ^ bits][...] for bits in range(4))
        out[56 * part : 56 * part + 56, :] = jnp.where(
            high_bit, jnp.where(low_bit, a, b), jnp.where(low_bit, c, d)
        )


def add_kernel(one, two, out, done):
    out[...] = one[...] + two[...]
    done[...] = one[0:8, :]


def unpack_kernel(core, own, other, after, out):
    odd = is_odd(core)
    for j in range(7):
        rows = slice(32 * j, 32 * j + 32)
        halves = (
            jnp.where(odd, other[rows, :], own[rows, :]),
            jnp.where(odd, own[rows, :], other[rows, :]),
        )
        for half in range(2):
            for k in range(2):
                tap = 14 * half + 2 * j + k
                if tap < 27:
                    out[tap, :, :] = halves[half][:, 64 * k : 64 * k + 64]


VMEM = pl.BlockSpec(memory_space=pltpu.VMEM)
SMEM = pl.BlockSpec(memory_space=pltpu.SMEM)
PARAMS = pltpu.CompilerParams(vmem_limit_bytes=40 * 2**20)


def shape(*dims, dtype=F32):
    return jax.ShapeDtypeStruct(dims, dtype)


def call(kernel, outs, in_specs, scratch=(), flops=0, moved=0):
    return pl.pallas_call(
        kernel,
        out_shape=outs,
        in_specs=in_specs,
        out_specs=jax.tree.map(lambda _: VMEM, outs),
        scratch_shapes=scratch,
        compiler_params=PARAMS,
        cost_estimate=pl.CostEstimate(flops=flops, bytes_accessed=moved, transcendentals=0),
    )


def crossed(value, bits):
    axis = ("z", "y", "xh")
    return lax.ppermute(value, axis, [(s, s ^ bits) for s in range(lax.axis_size(axis))])


def summed_near(keep, give):
    small = shape(56, 128)
    own, one, two, three = call(
        quarters_kernel, (small,) * 4, [SMEM, VMEM, VMEM], [pltpu.VMEM((224, 128), F32)]
    )(quarter_place(), keep, swapped(give, "c", 0))
    three, two, one = (crossed(v, bits) for v, bits in ((three, 10), (two, 8), (one, 2)))
    return call(sum_kernel, small, [VMEM] * 4)(three, two, one, own)


def summed_far(part):
    for steps in ((7, 1, 6), (32, 48, 16)):
        parts = [crossed(part, bits) for bits in steps]
        part = call(sum_kernel, shape(56, 128), [VMEM] * 4)(*parts, part)
    return part


def gathered(part, done):
    three, two, one = (crossed(part, bits) for bits in (10, 8, 2))
    half = call(join_kernel, shape(224, 128), [SMEM] + [VMEM] * 4)(
        quarter_place(), three, two, one, part
    )
    return call(unpack_kernel, shape(27, 32, 64), [SMEM, VMEM, VMEM, VMEM])(
        place("c"), half, swapped(half, "c", 0), done
    )


def quarter_place():
    y, z = place("y"), place("z")
    return ((y ^ (y >> 1)) & 1) + 2 * (z & 1)


def place(axis):
    return lax.axis_index(axis).astype(jnp.int32).reshape(1)


def body(activation, out_grad, kernel):
    act = activation.reshape(512, 128)
    grad = out_grad.reshape(512, 128)
    chan, along, across = place("chan"), place(ALONG_X), place(ALONG_Y)
    to_far, to_near = call(rows_kernel, (shape(128, 128),) * 2, [SMEM, VMEM])(along, grad)
    far_row = swapped(to_far, ALONG_X, 1)
    other = swapped(act, "chan", 0)
    near_row = swapped(to_near, ALONG_X, 0)
    to_chip, to_core = call(edges_kernel, (shape(CI, 128),) * 2, [SMEM] * 2 + [VMEM] * 3)(
        along, across, grad, far_row, near_row
    )
    from_chip = swapped(to_chip, ALONG_Y, 1)
    from_core = swapped(to_core, "c", 0)
    halves = [pltpu.VMEM((3, 6, CI, 768), BF16)] * 2
    column = shape(64, 128)
    total, first, last = call(
        filter_kernel, (shape(864, 64), column, column), [SMEM] * 2 + [VMEM] * 5, halves, 700_000_000, 1 << 22
    )(chan, along, act, other, grad, far_row, near_row)
    keep, give = call(rim_kernel, (shape(224, 128),) * 2, [SMEM] + [VMEM] * 5)(
        across, total, first, last, from_chip, from_core
    )
    part = summed_near(keep, give)
    kept, sent = call(
        data_kernel, (shape(512, 128),) * 2, [SMEM] * 3 + [VMEM] * 7, halves, 700_000_000, 1 << 22
    )(chan, along, across, part, kernel, grad, far_row, near_row, from_chip, from_core)
    part = summed_far(part)
    sent = call(gate_kernel, shape(512, 128), [VMEM] * 2)(sent, part)
    input_grad, done = call(add_kernel, (shape(512, 128), shape(8, 128)), [VMEM] * 2)(
        kept, swapped(sent, "chan", 0)
    )
    input_grad = input_grad.reshape(activation.shape)
    kernel_grad = gathered(part, done)
    return (input_grad, kernel_grad)


def solution(mesh):
    mesh = Mesh(mesh.devices.reshape(8, 4, 2, 2, 2), TILE + ("chan",))
    field = P("chan", TILE, None, None, None)
    weights = P(None, "chan", None)
    return jax.shard_map(
        body,
        mesh=mesh,
        in_specs=(field, field, weights),
        out_specs=(field, weights),
        check_vma=False,
    )
```

```python
import jax
import jax.numpy as jnp
from jax import lax
from jax.experimental import pallas as pl
from jax.experimental.pallas import tpu as pltpu
from jax.sharding import Mesh, PartitionSpec as P

F32, BF16 = jnp.float32, jnp.bfloat16
ALONG_X = ("z", "y")
ALONG_Y = ("xh", "c")
TILE = ALONG_X + ALONG_Y
CI = 32
NT = (((1,), (1,)), ((), ()))


def swapped(value, axis, first):
    count = lax.axis_size(axis)
    pairs = [(s, (s + 1) % count) for s in range(first, count, 2)]
    return lax.ppermute(value, axis, pairs + [(t, s) for s, t in pairs])


def split(value):
    high = value.astype(BF16)
    return high, (value - high.astype(F32)).astype(BF16)


def rows_kernel(along, grad, far, near):
    odd = is_odd(along)
    for z in range(4):
        top = grad[pl.ds(12 + z, CI, stride=16), :]
        bottom = grad[pl.ds(z, CI, stride=16), :]
        far[pl.ds(z, CI, stride=4), :] = jnp.where(odd, top, bottom)
        near[pl.ds(z, CI, stride=4), :] = jnp.where(odd, bottom, top)


def edges_kernel(along, across, grad, far_row, near_row, to_chip, to_core):
    lane = lax.broadcasted_iota(jnp.int32, (CI, 128), 1)
    heads = jnp.zeros((CI, 128), F32)
    tails = jnp.zeros((CI, 128), F32)
    for xp in range(6):
        for z in range(4):
            tile = extended(along, grad, far_row, near_row, xp, z)
            at = 6 * xp + z + 1
            heads = jnp.where(lane == at, pltpu.roll(tile, at, 1), heads)
            tails = jnp.where(lane == at, pltpu.roll(tile, at + 1, 1), tails)
    odd = is_odd(across)
    to_core[...] = jnp.where(odd, heads, tails)
    to_chip[...] = jnp.where(odd, tails, heads)


def extended(along, grad, far_row, near_row, xp, z):
    if 0 < xp < 5:
        return grad[pl.ds((xp - 1) * 4 + z, CI, stride=16), :]
    near = near_row[pl.ds(z, CI, stride=4), :]
    far = far_row[pl.ds(z, CI, stride=4), :]
    row = jnp.where(is_odd(along) == (xp == 0), near, far)
    return jnp.where(along[0] == (0 if xp == 0 else 31), 0.0, row)


def is_odd(place):
    return (place[0] & 1) == 1


def spread(along, grad, far_row, near_row, left, right, high, low):
    lane = lax.broadcasted_iota(jnp.int32, (CI, 128), 1)
    zero = jnp.zeros((CI, 128), BF16)
    for xp in range(6):
        for d in range(3):
            for ref in (high, low):
                ref[d, xp, :, 0:128] = zero
                ref[d, xp, :, 640:768] = zero
        for z in range(4):
            tile = extended(along, grad, far_row, near_row, xp, z)
            before, after = pltpu.roll(tile, 1, 1), pltpu.roll(tile, 127, 1)
            if left is None:
                before = jnp.where(lane == 0, 0.0, before)
                after = jnp.where(lane == 127, 0.0, after)
            else:
                at = 6 * xp + z + 1
                before = jnp.where(lane == 0, pltpu.roll(left, 128 - at, 1), before)
                after = jnp.where(lane == 127, pltpu.roll(right, 127 - at, 1), after)
            for d, value in ((0, after), (1, tile), (2, before)):
                high[d, xp, :, (z + 1) * 128 : (z + 2) * 128], low[
                    d, xp, :, (z + 1) * 128 : (z + 2) * 128
                ] = split(value)


def taps(ref, x):
    return jnp.concatenate(
        [
            ref[d, x + 2 - a, :, (2 - b) * 128 : (2 - b) * 128 + 512]
            for a in range(3)
            for b in range(3)
            for d in range(3)
        ],
        axis=0,
    )


def x_row(ref, x):
    return jnp.concatenate([ref[pl.ds(x * 4 + z, CI, stride=16), :] for z in range(4)], axis=1)


def filter_kernel(
    chan, along, own, other, grad, far_row, near_row, total_out, first_out, last_out, high, low
):
    spread(along, grad, far_row, near_row, None, None, high, low)
    is_first = chan[0] == 0
    lane = lax.broadcasted_iota(jnp.int32, (64, 128), 1)
    heads = jnp.zeros((64, 128), F32)
    tails = jnp.zeros((64, 128), F32)
    total = None
    for x in range(4):
        mine, theirs = x_row(own, x), x_row(other, x)
        act = jnp.concatenate(
            [jnp.where(is_first, mine, theirs), jnp.where(is_first, theirs, mine)], axis=0
        )
        for z in range(4):
            at, tile = 6 * x + z, act[:, 128 * z : 128 * z + 128]
            heads = jnp.where(lane == at, pltpu.roll(tile, at, 1) if at else tile, heads)
            tails = jnp.where(lane == at, pltpu.roll(tile, at + 1, 1), tails)
        act_high, act_low = split(act)
        both = jnp.concatenate([act_high, act_low], axis=0)
        p = lax.dot_general(taps(high, x), both, NT, preferred_element_type=F32)
        q = lax.dot_general(taps(low, x), act_high, NT, preferred_element_type=F32)
        part = p[:, :64] + p[:, 64:] + q
        total = part if total is None else total + part
    total_out[...] = total
    first_out[...] = heads
    last_out[...] = tails


def rims(across, from_chip, from_core):
    odd = is_odd(across)
    left = jnp.where(odd, from_core[...], from_chip[...])
    right = jnp.where(odd, from_chip[...], from_core[...])
    return jnp.where(across[0] == 0, 0.0, left), jnp.where(across[0] == 3, 0.0, right)


def rim_taps(rim, column):
    shifted = jnp.concatenate(
        [
            pltpu.roll(rim, 128 - (6 * (2 - a) + 2 - b), 1) if a + b < 4 else rim
            for a in range(3)
            for b in range(3)
        ],
        axis=0,
    )
    high, low = split(shifted)
    col_high, col_low = split(column)
    both = jnp.concatenate([col_high, col_low], axis=0)
    p = lax.dot_general(high, both, NT, preferred_element_type=F32)
    q = lax.dot_general(low, col_high, NT, preferred_element_type=F32)
    return p[:, :64] + p[:, 64:] + q


def rim_kernel(across, total, first, last, from_chip, from_core, keep, give):
    left, right = rims(across, from_chip, from_core)
    extra = {2: rim_taps(left, first[...]), 0: rim_taps(right, last[...])}

    def of_tap(tap):
        if tap > 26:
            return jnp.zeros((CI, 64), F32)
        value = total[CI * tap : CI * tap + CI, :]
        group, d = divmod(tap, 3)
        if d in extra:
            value = value + extra[d][CI * group : CI * group + CI]
        return value * (1.0 / 512.0)

    odd = is_odd(across)
    for j in range(7):
        pairs = [
            jnp.concatenate([of_tap(2 * pair), of_tap(2 * pair + 1)], axis=1)
            for pair in (j, j + 7)
        ]
        keep[32 * j : 32 * j + 32, :] = jnp.where(odd, pairs[1], pairs[0])
        give[32 * j : 32 * j + 32, :] = jnp.where(odd, pairs[0], pairs[1])


def data_kernel(
    chan, along, across, after, weights, grad, far_row, near_row, from_chip, from_core, kept, sent, high, low
):
    left, right = rims(across, from_chip, from_core)
    spread(along, grad, far_row, near_row, left, right, high, low)
    w = weights[...].reshape(864, 64)
    w = jnp.where(chan[0] == 0, w, jnp.concatenate([w[:, 32:], w[:, :32]], axis=1))
    w_high = w.astype(BF16).astype(F32)
    both = jnp.concatenate([w_high, w - w_high], axis=1)
    both = jnp.concatenate([both, jnp.zeros((32, 128), F32)], axis=0)
    both = both.T.astype(BF16)[:, :864]
    for x in range(4):
        p = jnp.dot(both, taps(high, x), preferred_element_type=F32)
        q = jnp.dot(both[:64], taps(low, x), preferred_element_type=F32)
        result = p[:64] + p[64:] + q
        for z in range(4):
            tile = result[:, z * 128 : (z + 1) * 128]
            kept[pl.ds(x * 4 + z, CI, stride=16), :] = tile[:32]
            sent[pl.ds(x * 4 + z, CI, stride=16), :] = tile[32:]


def quarter(ref, index):
    return ref[pl.ds(pl.multiple_of(index * 56, 8), 56), :]


def quarters_kernel(row, kept, received, own, one, two, three, both):
    both[...] = kept[...] + received[...]
    for bits, out in enumerate((own, one, two, three)):
        out[...] = quarter(both, row[0] ^ bits)


def sum_kernel(three, two, one, own, out):
    out[...] = (own[...] + one[...]) + (two[...] + three[...])


def join_kernel(row, three, two, one, own, out):
    low_bit, high_bit = (row[0] & 1) == 0, (row[0] & 2) == 0
    refs = (own, one, two, three)
    for part in range(4):
        a, b, c, d = (refs[part ^ bits][...] for bits in range(4))
        out[56 * part : 56 * part + 56, :] = jnp.where(
            high_bit, jnp.where(low_bit, a, b), jnp.where(low_bit, c, d)
        )


def add_kernel(one, two, out, done):
    out[...] = one[...] + two[...]
    done[...] = one[0:8, :]


def unpack_kernel(core, own, other, after, out):
    odd = is_odd(core)
    for j in range(7):
        rows = slice(32 * j, 32 * j + 32)
        halves = (
            jnp.where(odd, other[rows, :], own[rows, :]),
            jnp.where(odd, own[rows, :], other[rows, :]),
        )
        for half in range(2):
            for k in range(2):
                tap = 14 * half + 2 * j + k
                if tap < 27:
                    out[tap, :, :] = halves[half][:, 64 * k : 64 * k + 64]


VMEM = pl.BlockSpec(memory_space=pltpu.VMEM)
SMEM = pl.BlockSpec(memory_space=pltpu.SMEM)
PARAMS = pltpu.CompilerParams(vmem_limit_bytes=40 * 2**20)


def shape(*dims, dtype=F32):
    return jax.ShapeDtypeStruct(dims, dtype)


def call(kernel, outs, in_specs, scratch=(), flops=0, moved=0):
    return pl.pallas_call(
        kernel,
        out_shape=outs,
        in_specs=in_specs,
        out_specs=jax.tree.map(lambda _: VMEM, outs),
        scratch_shapes=scratch,
        compiler_params=PARAMS,
        cost_estimate=pl.CostEstimate(flops=flops, bytes_accessed=moved, transcendentals=0),
    )


def crossed(value, bits):
    axis = ("z", "y", "xh")
    return lax.ppermute(value, axis, [(s, s ^ bits) for s in range(lax.axis_size(axis))])


def summed_near(keep, give):
    small = shape(56, 128)
    own, one, two, three = call(
        quarters_kernel, (small,) * 4, [SMEM, VMEM, VMEM], [pltpu.VMEM((224, 128), F32)]
    )(quarter_place(), keep, swapped(give, "c", 0))
    three, two, one = (crossed(v, bits) for v, bits in ((three, 10), (two, 8), (one, 2)))
    return call(sum_kernel, small, [VMEM] * 4)(three, two, one, own)


def summed_over(part, steps):
    parts = [crossed(part, bits) for bits in steps]
    return call(sum_kernel, shape(56, 128), [VMEM] * 4)(*parts, part)


def gathered(part, done):
    three, two, one = (crossed(part, bits) for bits in (10, 8, 2))
    half = call(join_kernel, shape(224, 128), [SMEM] + [VMEM] * 4)(
        quarter_place(), three, two, one, part
    )
    return call(unpack_kernel, shape(27, 32, 64), [SMEM, VMEM, VMEM, VMEM])(
        place("c"), half, swapped(half, "c", 0), done
    )


def quarter_place():
    y, z = place("y"), place("z")
    return ((y ^ (y >> 1)) & 1) + 2 * (z & 1)


def place(axis):
    return lax.axis_index(axis).astype(jnp.int32).reshape(1)


def body(activation, out_grad, kernel):
    act = activation.reshape(512, 128)
    grad = out_grad.reshape(512, 128)
    chan, along, across = place("chan"), place(ALONG_X), place(ALONG_Y)
    to_far, to_near = call(rows_kernel, (shape(128, 128),) * 2, [SMEM, VMEM])(along, grad)
    far_row = swapped(to_far, ALONG_X, 1)
    other = swapped(act, "chan", 0)
    near_row = swapped(to_near, ALONG_X, 0)
    to_chip, to_core = call(edges_kernel, (shape(CI, 128),) * 2, [SMEM] * 2 + [VMEM] * 3)(
        along, across, grad, far_row, near_row
    )
    from_chip = swapped(to_chip, ALONG_Y, 1)
    from_core = swapped(to_core, "c", 0)
    halves = [pltpu.VMEM((3, 6, CI, 768), BF16)] * 2
    column = shape(64, 128)
    total, first, last = call(
        filter_kernel, (shape(864, 64), column, column), [SMEM] * 2 + [VMEM] * 5, halves, 700_000_000, 1 << 22
    )(chan, along, act, other, grad, far_row, near_row)
    keep, give = call(rim_kernel, (shape(224, 128),) * 2, [SMEM] + [VMEM] * 5)(
        across, total, first, last, from_chip, from_core
    )
    part = summed_near(keep, give)
    kept, sent = call(
        data_kernel, (shape(512, 128),) * 2, [SMEM] * 3 + [VMEM] * 7, halves, 700_000_000, 1 << 22
    )(chan, along, across, part, kernel, grad, far_row, near_row, from_chip, from_core)
    part = summed_over(part, (7, 1, 6))
    part, sent = lax.optimization_barrier((part, sent))
    input_grad, done = call(add_kernel, (shape(512, 128), shape(8, 128)), [VMEM] * 2)(
        kept, swapped(sent, "chan", 0)
    )
    part = summed_over(part, (32, 48, 16))
    input_grad = input_grad.reshape(activation.shape)
    kernel_grad = gathered(part, done)
    return (input_grad, kernel_grad)


def solution(mesh):
    mesh = Mesh(mesh.devices.reshape(8, 4, 2, 2, 2), TILE + ("chan",))
    field = P("chan", TILE, None, None, None)
    weights = P(None, "chan", None)
    return jax.shard_map(
        body,
        mesh=mesh,
        in_specs=(field, field, weights),
        out_specs=(field, weights),
        check_vma=False,
    )
```
